32 devices in a mesh: dp: 4 (over z), fsdp: 8 (over y, x, core).
Axes of the slice: x: 2, y: 2, z: 4, core: 2. Of those that a mesh axis runs over, the one named last changes fastest.
Arguments:
- latents: bfloat16 [32, 320, 16], P(('dp', 'fsdp')), may hold values from -6 to 6
- noise: float32 [32, 320, 16], P(('dp', 'fsdp')), may hold values from -6 to 6
- lengths: int32 [32], P(('dp', 'fsdp')), may hold values from 192 to 320, as said below
- timesteps: int32 [32], P(('dp', 'fsdp')), may hold values from 0 to 999
- labels: int32 [32], P(('dp', 'fsdp')), may hold values from 0 to 1000
- enc_feats: float32 [32, 768], P(('dp', 'fsdp')), may hold values from -6 to 6
- pair_idx: int32 [32], P(('dp', 'fsdp')), may hold values from 0 to 31
- step: int32 [1], replicated, may hold values from 2 to 20
- rows_w: float32 [3, 9216, 1152], P(None, ('dp', 'fsdp'))
- fc2_w: float32 [3, 4608, 1152], P(None, ('dp', 'fsdp')), may hold values from -0.09375 to 0.09375
- misc_w: float32 [5101056], P(('dp', 'fsdp'))
- gains: float32 [16128], P(('dp', 'fsdp'))
- rows_m: float32 [3, 9216, 1152], P(None, ('dp', 'fsdp')), may hold values from -2.3841858e-06 to 2.3841858e-06
- rows_v: float32 [3, 9216, 1152], P(None, ('dp', 'fsdp')), may hold values from 1.0020243e-13 to 3.970285e-13
- fc2_m: float32 [3, 4608, 1152], P(None, ('dp', 'fsdp')), may hold values from -2.3841858e-06 to 2.3841858e-06
- fc2_v: float32 [3, 4608, 1152], P(None, ('dp', 'fsdp')), may hold values from 1.0020243e-13 to 3.970285e-13
- misc_m: float32 [5101056], P(('dp', 'fsdp')), may hold values from -2.3841858e-06 to 2.3841858e-06
- misc_v: float32 [5101056], P(('dp', 'fsdp')), may hold values from 3.0249791e-12 to 1.20999166e-11
- gains_m: float32 [16128], P(('dp', 'fsdp')), may hold values from -2.2888184e-05 to 2.2888184e-05
- gains_v: float32 [16128], P(('dp', 'fsdp')), may hold values from 1.0020243e-11 to 3.970285e-11
Outputs:
- loss: float32 [], replicated
- grad_norm: float32 [], replicated
- rows_new: float32 [3, 9216, 1152], P(None, ('dp', 'fsdp'))
- rows_m_new: float32 [3, 9216, 1152], P(None, ('dp', 'fsdp'))
- rows_v_new: float32 [3, 9216, 1152], P(None, ('dp', 'fsdp'))
- rows_low: bfloat16 [3, 9216, 1152], P(None, ('dp', 'fsdp'))
- fc2_new: float32 [3, 4608, 1152], P(None, ('dp', 'fsdp'))
- fc2_m_new: float32 [3, 4608, 1152], P(None, ('dp', 'fsdp'))
- fc2_v_new: float32 [3, 4608, 1152], P(None, ('dp', 'fsdp'))
- fc2_low: bfloat16 [3, 4608, 1152], P(None, ('dp', 'fsdp'))
- misc_new: float32 [5101056], P(('dp', 'fsdp'))
- misc_m_new: float32 [5101056], P(('dp', 'fsdp'))
- misc_v_new: float32 [5101056], P(('dp', 'fsdp'))
- misc_low: bfloat16 [5101056], P(('dp', 'fsdp'))
- gains_new: float32 [16128], P(('dp', 'fsdp'))
- gains_m_new: float32 [16128], P(('dp', 'fsdp'))
- gains_v_new: float32 [16128], P(('dp', 'fsdp'))
- gains_low: bfloat16 [16128], P(('dp', 'fsdp'))
- norms: float32 [19, 2], replicated
The draws below stay inside these ranges and needn't reach their ends.
Inputs may be any that keep to these rules, and one draw needn't show every extreme that they name: `lengths`: live patches of an item; patch slot j is live where j < the length; in every draw some item has 320 and another 192.
All inputs are finite; a program needn't handle non-finite values.
Results may differ from the reference program's by a relative error of at most 0.012.
The reference program's roundings to bfloat16 on the way (of `weights`) count: a program that leaves them out, or rounds other values in their place, can miss the bound.
Values may be sent and summed in bfloat16 or wider, within the bound.
A program may use at most 576 MiB of HBM per device.

```python
import math
import jax
import jax.numpy as jnp
from jax import lax

D = 1152
H = 16
HD = 72
FF = 4608
PIN = 16
ENC = 768
CLS = 1001
L = 322
MINLEN = 192
BLOCKS = 3
PATCH = 320
ITEMS = 32
RW = 9216
P_MISC = 5101056
GN = 16128
NPARAM = 52892928


def draw_lengths(key, part):
    lengths_drawn = jax.random.randint(key, (ITEMS,), MINLEN, PATCH + 1)
    first_item = jax.random.randint(jax.random.fold_in(key, 1), (), 0, ITEMS)
    second_item = (first_item + 1 + jax.random.randint(jax.random.fold_in(key, 2), (), 0, ITEMS - 1)) % ITEMS
    item_index = jnp.arange(ITEMS)
    lengths_drawn = jnp.where(item_index == first_item, PATCH, lengths_drawn)
    lengths_drawn = jnp.where(item_index == second_item, MINLEN, lengths_drawn)
    return lengths_drawn.astype(jnp.int32)


def draw_rows_w(key, part):
    drawn = jax.random.normal(key, (BLOCKS, 4 * D + FF, D), jnp.float32) * D ** (-0.5)
    column = jnp.arange(4 * D + FF)
    factor = jnp.where((column >= 3 * D) & (column < 4 * D), 4.0, 1.0)
    return drawn * factor[None, :, None]


def draw_misc_w(key, part):
    section_sizes = [(PIN + 1) * D, D * PIN, L * D, CLS * D, 2 * D * D, D * ENC]
    section_scales = [PIN ** (-0.5), D ** (-0.5), 0.02, 0.03, (2 * D) ** (-0.5), D ** (-0.5)]
    count_all = sum(section_sizes)
    position = jnp.arange(count_all)
    factor = jnp.full((count_all,), section_scales[0], jnp.float32)
    offset = 0
    for length, factor_now in zip(section_sizes, section_scales):
        factor = jnp.where(position >= offset, factor_now, factor)
        offset += length
    return jax.random.normal(key, (count_all,), jnp.float32) * factor


def draw_gains(key, part):
    row_count = 4 * BLOCKS + 2
    row_index = jnp.arange(row_count)[:, None]
    gain_rows = jax.random.uniform(jax.random.fold_in(key, 1), (row_count, D), jnp.float32, 0.6, 1.4)
    bias_rows = jax.random.normal(jax.random.fold_in(key, 2), (row_count, D), jnp.float32) * 0.3
    return jnp.where(row_index % 2 == 0, gain_rows, bias_rows).reshape(-1)


def set_ends(entries, key, least, top_value):
    longest = entries.shape.index(max(entries.shape))
    spots = []
    for shift in (0, 1):
        where = [jax.random.randint(jax.random.fold_in(key, axis), (), 0, length) for axis, length in enumerate(entries.shape)]
        where[longest] = (where[longest] + shift) % entries.shape[longest]
        spots.append(tuple(where))
    return entries.at[spots[0]].set(least).at[spots[1]].set(top_value)


def levels(key, shape, cuts, smallest, largest):
    loudness = 1.0
    for axis_at, blocks in cuts:
        heights = jax.random.uniform(jax.random.fold_in(jax.random.fold_in(key, 6), axis_at), (blocks,), jnp.float32, smallest / len(cuts), largest / len(cuts))
        loudness = loudness * jnp.repeat(jnp.exp(heights), shape[axis_at] // blocks).reshape((-1,) + (1,) * (len(shape) - 1 - axis_at))
    return loudness


def bell_draw(own_key, dims, scale, reach, cuts=(), kind=jnp.bfloat16):
    values = scale * jax.random.normal(own_key, dims, jnp.float32)
    if cuts:
        values = values * levels(own_key, dims, cuts, -0.22, 0.18)
    return jnp.clip(values, -reach, reach).astype(kind)


def setup_inputs(seed: int = 0) -> dict:
    seeds = jax.random.split(jax.random.key(seed), 21)
    latents = bell_draw(seeds[0], (ITEMS, PATCH, PIN), 1.0, 6.0, ((0, 32),))
    noise = bell_draw(seeds[1], (ITEMS, PATCH, PIN), 1.0, 6.0, ((0, 32),), jnp.float32)
    lengths = draw_lengths(jax.random.fold_in(seeds[20], 71), 0)
    timesteps = set_ends(jax.random.randint(seeds[3], (ITEMS,), 0, 1000), jax.random.fold_in(seeds[3], 1), 0, 999).astype(jnp.int32)
    labels = set_ends(jax.random.randint(seeds[4], (ITEMS,), 0, CLS), jax.random.fold_in(seeds[4], 1), 0, CLS - 1).astype(jnp.int32)
    enc_feats = bell_draw(seeds[5], (ITEMS, ENC), 1.0, 6.0, ((0, 32),), jnp.float32)
    pair_idx = set_ends(jax.random.randint(seeds[6], (ITEMS,), 0, ITEMS), jax.random.fold_in(seeds[6], 1), 0, ITEMS - 1).astype(jnp.int32)
    step = jax.random.randint(seeds[7], (1,), 2, 21).astype(jnp.int32)
    rows_w = draw_rows_w(jax.random.fold_in(seeds[20], 71), 0)
    fc2_w = bell_draw(seeds[9], (BLOCKS, FF, D), FF ** -0.5, 0.09375, ((1, 32),), jnp.float32)
    misc_w = draw_misc_w(jax.random.fold_in(seeds[20], 71), 0)
    gains = draw_gains(jax.random.fold_in(seeds[20], 71), 0)
    rows_m = bell_draw(seeds[12], (BLOCKS, RW, D), (0.0011 / NPARAM ** 0.5), 2.384185791015625e-06, ((1, 32),), jnp.float32)
    rows_v = jnp.clip(jnp.exp(math.log(3.970284929814827e-13) - 1.3768156 * jax.random.uniform(seeds[13], (BLOCKS, RW, D), jnp.float32) ** levels(seeds[13], (BLOCKS, RW, D), ((1, 32),), -0.2, 0.2)), 1.002024323432972e-13, 3.970284929814827e-13)
    fc2_m = bell_draw(seeds[14], (BLOCKS, FF, D), (0.0011 / NPARAM ** 0.5), 2.384185791015625e-06, ((1, 32),), jnp.float32)
    fc2_v = jnp.clip(jnp.exp(math.log(3.970284929814827e-13) - 1.3768156 * jax.random.uniform(seeds[15], (BLOCKS, FF, D), jnp.float32) ** levels(seeds[15], (BLOCKS, FF, D), ((1, 32),), -0.2, 0.2)), 1.002024323432972e-13, 3.970284929814827e-13)
    misc_m = bell_draw(seeds[16], (P_MISC,), (0.0011 / NPARAM ** 0.5), 2.384185791015625e-06, ((0, 32),), jnp.float32)
    misc_v = jnp.clip(jnp.exp(math.log(1.2099916554819679e-11) - 1.3862944 * jax.random.uniform(seeds[17], (P_MISC,), jnp.float32) ** levels(seeds[17], (P_MISC,), ((0, 32),), -0.2, 0.2)), 3.0249791387049196e-12, 1.2099916554819679e-11)
    gains_m = bell_draw(seeds[18], (GN,), (0.011 / NPARAM ** 0.5), 2.288818359375e-05, ((0, 32),), jnp.float32)
    gains_v = jnp.clip(jnp.exp(math.log(3.9702848647626965e-11) - 1.3768156 * jax.random.uniform(seeds[19], (GN,), jnp.float32) ** levels(seeds[19], (GN,), ((0, 32),), -0.2, 0.2)), 1.0020243315644883e-11, 3.9702848647626965e-11)
    return {"latents": latents, "noise": noise, "lengths": lengths, "timesteps": timesteps, "labels": labels, "enc_feats": enc_feats, "pair_idx": pair_idx, "step": step, "rows_w": rows_w, "fc2_w": fc2_w, "misc_w": misc_w, "gains": gains, "rows_m": rows_m, "rows_v": rows_v, "fc2_m": fc2_m, "fc2_v": fc2_v, "misc_m": misc_m, "misc_v": misc_v, "gains_m": gains_m, "gains_v": gains_v}


logit_softening_scale = 0.02
align_weight = 0.5
clip_limit = 0.01
beta_first = 0.9
beta_second = 0.95
learn_rate = 0.3
weight_decay = 0.01
adam_eps = 1e-08
layer_eps = 1e-05
vector_eps = 1e-06
mask_fill = -1e+30

@jax.custom_vjp
def low(v):
    return lax.optimization_barrier(v.astype(jnp.bfloat16)).astype(jnp.float32)

@jax.custom_vjp
def lowbit_reverse_pass(v):
    return v

def low_keep(v):
    return (low(v), None)

def low_pass(kept, grad):
    return (grad,)

def back_keep(v):
    return (v, None)

def back_low(kept, grad):
    return (low(grad),)
low.defvjp(low_keep, low_pass)
lowbit_reverse_pass.defvjp(back_keep, back_low)

def strict_multiply_option(form, left, right):
    return jnp.einsum(form, left, right, precision=lax.Precision.HIGHEST, preferred_element_type=jnp.float32)

def misc_bounds():
    return [(PIN + 1) * D, D * PIN, L * D, CLS * D, 2 * D * D, D * ENC]

def split_misc(flat):
    shapes = [(PIN + 1, D), (D, PIN), (L, D), (CLS, D), (2 * D, D), (D, ENC)]
    pieces = []
    offset = 0
    for shape_now in shapes:
        length = shape_now[0] * shape_now[1]
        pieces.append(flat[offset:offset + length].reshape(shape_now))
        offset += length
    return pieces

def time_embed(timesteps):
    half_width = D // 2
    frequency = jnp.exp(-math.log(10000.0) * jnp.arange(half_width).astype(jnp.float32) / half_width)
    angles = timesteps.astype(jnp.float32)[:, None] * frequency[None, :]
    return jnp.concatenate([jnp.cos(angles), jnp.sin(angles)], axis=-1)

def layer_norm(values, gain, bias):
    centered = values - lax.optimization_barrier(jnp.mean(values, axis=-1, keepdims=True))
    scale_inv = lax.rsqrt(lax.optimization_barrier(jnp.mean(centered * centered, axis=-1, keepdims=True)) + layer_eps)
    return centered * scale_inv * gain + bias

def block_forward(hidden, rows, fc2, gvec, keymask):
    count_items = hidden.shape[0]
    normed = low(layer_norm(hidden, gvec[0], gvec[1]))
    triple = low(lowbit_reverse_pass(strict_multiply_option('gld,ed->gle', normed, rows[:3 * D])))
    triple = triple.reshape(count_items, L, 3, H, HD)
    scores = lowbit_reverse_pass(strict_multiply_option('glhd,gmhd->ghlm', triple[:, :, 0], triple[:, :, 1]) * HD ** (-0.5))
    scores = jnp.where(keymask[:, None, None, :], scores, mask_fill)
    probs = low(jax.nn.softmax(scores, axis=-1))
    attended = strict_multiply_option('ghlm,gmhd->glhd', probs, triple[:, :, 2]).reshape(count_items, L, D)
    attended = low(lowbit_reverse_pass(attended))
    after = hidden + lowbit_reverse_pass(strict_multiply_option('gld,ed->gle', attended, rows[3 * D:4 * D]))
    normed_two = low(layer_norm(after, gvec[2], gvec[3]))
    inner = lowbit_reverse_pass(strict_multiply_option('gld,fd->glf', normed_two, rows[4 * D:]))
    active = low(jax.nn.gelu(inner, approximate=True))
    return after + lowbit_reverse_pass(strict_multiply_option('glf,fd->gld', active, fc2))

def group_forward(rows, fc2, misc, gain_flat, latents, noise, lengths, timesteps, labels):
    embed, head, posit, table, skip, align = split_misc(misc)
    gain_rows = gain_flat.reshape(-1, D)
    keymask = jnp.arange(L)[None, :] < lengths[:, None] + 2
    valid = (jnp.arange(PATCH)[None, :] < lengths[:, None]).astype(jnp.float32)
    live_count = lengths.astype(jnp.float32)
    patches = lowbit_reverse_pass(strict_multiply_option('gpc,cd->gpd', latents, embed[:PIN])) + embed[PIN]
    onehot = (labels[:, None] == jnp.arange(CLS)[None, :]).astype(jnp.float32)
    class_rows = strict_multiply_option('gc,cd->gd', onehot, table)
    hidden = jnp.concatenate([time_embed(timesteps)[:, None], class_rows[:, None], patches], axis=1) + posit[None]
    shallow = block_forward(hidden, rows[0], fc2[0], gain_rows[0:4], keymask)
    middle = block_forward(shallow, rows[1], fc2[1], gain_rows[4:8], keymask)
    joined = low(jnp.concatenate([middle, shallow], axis=-1))
    deep_in = lowbit_reverse_pass(strict_multiply_option('gle,ed->gld', joined, skip))
    deep = block_forward(deep_in, rows[2], fc2[2], gain_rows[8:12], keymask)
    final = low(layer_norm(deep[:, 2:], gain_rows[12], gain_rows[13]))
    pred = lowbit_reverse_pass(strict_multiply_option('gpd,dc->gpc', final, head))
    error = (pred - noise) ** 2 * valid[:, :, None]
    mse_sum = jnp.sum(lax.optimization_barrier(jnp.sum(error, axis=(1, 2))) / (live_count * PIN))
    pooled = low(lax.optimization_barrier(jnp.sum(middle[:, 2:] * valid[:, :, None], axis=1)) / live_count[:, None])
    projected = lowbit_reverse_pass(strict_multiply_option('gd,de->ge', pooled, align))
    zhat = projected * lax.rsqrt(lax.optimization_barrier(jnp.sum(projected * projected, axis=-1, keepdims=True)) + vector_eps)
    return (mse_sum, zhat)

def segment_kinds(rank_here, cols_here, misc_here):
    column = rank_here * cols_here + jnp.arange(cols_here)
    column_kind = (column >= 3 * D).astype(jnp.int32) + (column >= 4 * D).astype(jnp.int32)
    flat_index = rank_here * misc_here + jnp.arange(misc_here)
    misc_kind = jnp.zeros((misc_here,), jnp.int32)
    offset = 0
    for length in misc_bounds()[:-1]:
        offset += length
        misc_kind = misc_kind + (flat_index >= offset).astype(jnp.int32)
    return (column_kind, misc_kind)

def squares(kinds, rows, fc2, misc, gain_flat):
    column_kind, misc_kind = kinds
    column_sums = lax.optimization_barrier(jnp.sum(rows * rows, axis=2))
    rows_part = jnp.stack([lax.optimization_barrier(jnp.sum(jnp.where(column_kind == segment, column_sums, 0.0), axis=1)) for segment in range(3)], axis=1).reshape(-1)
    fc2_part = lax.optimization_barrier(jnp.sum(fc2 * fc2, axis=(1, 2)))
    misc_part = jnp.stack([jnp.sum(jnp.where(misc_kind == segment, misc * misc, 0.0)) for segment in range(6)])
    return jnp.concatenate([rows_part, fc2_part, misc_part, jnp.sum(gain_flat * gain_flat)[None]])

def spread(ratios, kinds, blocks):
    column_kind, misc_kind = kinds
    rows_map = ratios[3 * jnp.arange(blocks)[:, None, None] + column_kind[None, :, None]]
    fc2_map = ratios[3 * blocks + jnp.arange(blocks)][:, None, None]
    misc_map = ratios[4 * blocks + misc_kind]
    return (rows_map, fc2_map, misc_map, ratios[4 * blocks + 6])

def adam_move(grad, weight, first, second, factor, count, decay_now):
    clipped = factor * grad
    first_new = beta_first * first + (1.0 - beta_first) * clipped
    second_new = beta_second * second + (1.0 - beta_second) * clipped * clipped
    first_hat = first_new / (1.0 - beta_first ** count)
    second_hat = second_new / (1.0 - beta_second ** count)
    return (first_new, second_new, first_hat / (jnp.sqrt(second_hat) + adam_eps) + decay_now * weight)

def reference(latents, noise, lengths, timesteps, labels, enc_feats, pair_idx, step, rows_w, fc2_w, misc_w, gains, rows_m, rows_v, fc2_m, fc2_v, misc_m, misc_v, gains_m, gains_v):
    group_items = min(8, ITEMS)
    groups = ITEMS // group_items

    def regroup(array):
        return array.reshape((groups, group_items) + array.shape[1:])
    slabs = (regroup(latents.astype(jnp.float32)), regroup(noise), regroup(lengths), regroup(timesteps), regroup(labels))

    def loss_fn(rows, fc2, misc, gain_flat):
        rows_low = low(rows)
        fc2_low = low(fc2)
        misc_low = low(misc)
        gain_low = low(gain_flat)
        forward = jax.checkpoint(group_forward)

        def one_group(slab):
            return forward(rows_low, fc2_low, misc_low, gain_low, slab[0], slab[1], slab[2], slab[3], slab[4])
        mse_parts, zhat = lax.map(one_group, slabs)
        mse = jnp.sum(mse_parts) / ITEMS
        whole_embedding_table = low(zhat.reshape(ITEMS, ENC))
        normalised_latent_embeddings = low(enc_feats * lax.rsqrt(lax.optimization_barrier(jnp.sum(enc_feats * enc_feats, axis=-1, keepdims=True)) + vector_eps))
        cosine_score_table = lowbit_reverse_pass(strict_multiply_option('lj,yj->ly', normalised_latent_embeddings, whole_embedding_table) / logit_softening_scale)
        summed = jax.nn.logsumexp(cosine_score_table, axis=-1)
        picked = jnp.take_along_axis(cosine_score_table, pair_idx[:, None].astype(jnp.int32), axis=1)[:, 0]
        return mse + align_weight * jnp.mean(summed - picked)
    loss, pullback = jax.vjp(loss_fn, rows_w, fc2_w, misc_w, gains)
    grads = pullback(jnp.ones((), jnp.float32))
    weights = (rows_w, fc2_w, misc_w, gains)
    firsts = (rows_m, fc2_m, misc_m, gains_m)
    seconds = (rows_v, fc2_v, misc_v, gains_v)
    kinds = segment_kinds(0, rows_w.shape[1], misc_w.shape[0])
    grad_squares = squares(kinds, grads[0], grads[1], grads[2], grads[3])
    weight_squares = squares(kinds, rows_w, fc2_w, misc_w, gains)
    grad_norm = jnp.sqrt(jnp.sum(grad_squares))
    factor = jnp.minimum(1.0, clip_limit / grad_norm)
    count = step[0].astype(jnp.float32)
    moved = [adam_move(grads[member], weights[member], firsts[member], seconds[member], factor, count, weight_decay if member < 3 else 0.0) for member in range(4)]
    updates = [entry[2] for entry in moved]
    update_squares = squares(kinds, updates[0], updates[1], updates[2], updates[3])
    ratios = jnp.sqrt(weight_squares) / jnp.sqrt(update_squares + vector_eps)
    ratio_maps = spread(ratios, kinds, BLOCKS)
    renewed = [weights[member] - learn_rate * ratio_maps[member] * updates[member] for member in range(4)]
    norms = jnp.stack([jnp.sqrt(weight_squares), jnp.sqrt(update_squares)], axis=1)
    return (loss, grad_norm, renewed[0], moved[0][0], moved[0][1], renewed[0].astype(jnp.bfloat16), renewed[1], moved[1][0], moved[1][1], renewed[1].astype(jnp.bfloat16), renewed[2], moved[2][0], moved[2][1], renewed[2].astype(jnp.bfloat16), renewed[3], moved[3][0], moved[3][1], renewed[3].astype(jnp.bfloat16), norms)
```

```python
import functools
import math

import jax
import jax.numpy as jnp
from jax import lax
from jax.experimental import pallas as pl
from jax.experimental.pallas import tpu as pltpu
from jax.sharding import PartitionSpec as P

D = 1152
H = 16
HD = 72
PIN = 16
ENC = 768
CLS = 1001
L = 322
BLOCKS = 3
PATCH = 320


logit_softening_scale = 0.02
align_weight = 0.5
clip_limit = 0.01
beta_first = 0.9
beta_second = 0.95
learn_rate = 0.3
weight_decay = 0.01
adam_eps = 1e-08
layer_eps = 1e-05
vector_eps = 1e-06
mask_fill = -1e30


def misc_bounds():
    return [(PIN + 1) * D, D * PIN, L * D, CLS * D, 2 * D * D, D * ENC]


def split_misc(flat):
    shapes = [(PIN + 1, D), (D, PIN), (L, D), (CLS, D), (2 * D, D), (D, ENC)]
    pieces = []
    offset = 0
    for shape_now in shapes:
        length = shape_now[0] * shape_now[1]
        pieces.append(flat[offset : offset + length].reshape(shape_now))
        offset += length
    return pieces


def time_embed(timesteps):
    half_width = D // 2
    frequency = jnp.exp(
        -math.log(10000.0) * jnp.arange(half_width).astype(jnp.float32) / half_width
    )
    angles = timesteps.astype(jnp.float32)[:, None] * frequency[None, :]
    return jnp.concatenate([jnp.cos(angles), jnp.sin(angles)], axis=-1)


def collected_sample_embeddings(left, right):
    return lax.dot_general(
        left.reshape(-1, left.shape[-1]),
        right.reshape(-1, right.shape[-1]),
        (((0,), (0,)), ((), ())),
        preferred_element_type=jnp.float32,
    )


def gram_crossing(left, right):
    return lax.dot_general(
        left, right, (((left.ndim - 1,), (1,)), ((), ())), preferred_element_type=jnp.float32
    )


def layer_norm(values, gain, bias):
    centered = values - jnp.mean(values, axis=-1, keepdims=True)
    scale_inv = lax.rsqrt(jnp.mean(centered * centered, axis=-1, keepdims=True) + layer_eps)
    normal = centered * scale_inv
    return (normal * gain + bias, (normal, scale_inv))


def norm_back(grad, saved, gain):
    normal, scale_inv = saved
    dnormal = grad * gain
    dvalues = scale_inv * (
        dnormal
        - jnp.mean(dnormal, axis=-1, keepdims=True)
        - normal * jnp.mean(dnormal * normal, axis=-1, keepdims=True)
    )
    dgain = jnp.sum((grad * normal).reshape(-1, grad.shape[-1]), axis=0)
    dbias = jnp.sum(grad.reshape(-1, grad.shape[-1]), axis=0)
    return (dvalues, dgain, dbias)


def split_heads(triple):
    shaped = triple.reshape(triple.shape[0], triple.shape[1], 3, H, HD)
    return (shaped[:, :, 0], shaped[:, :, 1], shaped[:, :, 2])


def attend_scores(queries, keys_all, keymask):
    scores = jnp.einsum(
        "ilhd,imhd->ihlm", queries, keys_all, preferred_element_type=jnp.float32
    ) * HD ** (-0.5)
    return jnp.where(keymask[:, None, None, :], scores, mask_fill)


def attend_forward(triple, keymask):
    queries, keys_all, values = split_heads(triple)
    scores = attend_scores(queries, keys_all, keymask)
    highest = jnp.max(scores, axis=-1, keepdims=True)
    logsum = highest + jnp.log(jnp.sum(jnp.exp(scores - highest), axis=-1, keepdims=True))
    probs = jnp.exp(scores - logsum).astype(jnp.bfloat16)
    attended = jnp.einsum("ihlm,imhd->ilhd", probs, values, preferred_element_type=jnp.float32)
    return (attended.reshape(triple.shape[0], triple.shape[1], H * HD).astype(jnp.bfloat16), logsum)


def attend_backward(dattended, triple, logsum, keymask):
    queries, keys_all, values = split_heads(triple)
    probs = jnp.exp(attend_scores(queries, keys_all, keymask) - logsum)
    dout = dattended.reshape(dattended.shape[0], dattended.shape[1], H, HD)
    dprobs = jnp.einsum("ilhd,imhd->ihlm", dout, values, preferred_element_type=jnp.float32)
    dscores = (probs * (dprobs - jnp.sum(probs * dprobs, axis=-1, keepdims=True))).astype(
        jnp.bfloat16
    )
    dqueries = jnp.einsum(
        "ihlm,imhd->ilhd", dscores, keys_all, preferred_element_type=jnp.float32
    ) * HD ** (-0.5)
    dkeys = jnp.einsum(
        "ihlm,ilhd->imhd", dscores, queries, preferred_element_type=jnp.float32
    ) * HD ** (-0.5)
    dvalues = jnp.einsum(
        "ihlm,ilhd->imhd", probs.astype(jnp.bfloat16), dout, preferred_element_type=jnp.float32
    )
    joined = jnp.stack([dqueries, dkeys, dvalues], axis=2)
    return joined.reshape(triple.shape).astype(jnp.bfloat16)


def block_forward(hidden, rows, fc2, gvec, keymask):
    normed, save_one = layer_norm(hidden, gvec[0], gvec[1])
    normed_low = normed.astype(jnp.bfloat16)
    triple = gram_crossing(normed_low, rows[: 3 * D]).astype(jnp.bfloat16)
    attended, logsum = attend_forward(triple, keymask)
    after = hidden + gram_crossing(attended, rows[3 * D : 4 * D])
    normed_two, save_two = layer_norm(after, gvec[2], gvec[3])
    normed_two_low = normed_two.astype(jnp.bfloat16)
    inner = gram_crossing(normed_two_low, rows[4 * D :])
    active = jax.nn.gelu(inner, approximate=True).astype(jnp.bfloat16)
    output = after + jnp.dot(active, fc2, preferred_element_type=jnp.float32)
    return (
        output,
        (save_one, normed_low, triple, logsum, attended, save_two, normed_two_low, inner, active),
    )


def block_backward(dout, rows, fc2, gvec, keymask, saved):
    save_one, normed_low, triple, logsum, attended, save_two, normed_two_low, inner, active = saved
    dlow = dout.astype(jnp.bfloat16)
    grad_fc2 = collected_sample_embeddings(active, dlow)
    dactive = gram_crossing(dlow, fc2)
    slope = jax.vjp(lambda entry: jax.nn.gelu(entry, approximate=True), inner)[1](dactive)[0]
    dinner = slope.astype(jnp.bfloat16)
    grad_first = collected_sample_embeddings(dinner, normed_two_low)
    dnormed_two = jnp.dot(dinner, rows[4 * D :], preferred_element_type=jnp.float32)
    dafter_norm, dgain_two, dbias_two = norm_back(dnormed_two, save_two, gvec[2])
    dafter = dout + dafter_norm
    dafter_low = dafter.astype(jnp.bfloat16)
    grad_out = collected_sample_embeddings(dafter_low, attended)
    dattended = jnp.dot(dafter_low, rows[3 * D : 4 * D], preferred_element_type=jnp.float32).astype(
        jnp.bfloat16
    )
    dtriple = attend_backward(dattended, triple, logsum, keymask)
    grad_triple = collected_sample_embeddings(dtriple, normed_low)
    dnormed = jnp.dot(dtriple, rows[: 3 * D], preferred_element_type=jnp.float32)
    dhidden_norm, dgain_one, dbias_one = norm_back(dnormed, save_one, gvec[0])
    grad_rows = jnp.concatenate([grad_triple, grad_out, grad_first], axis=0)
    gain_grad = jnp.stack([dgain_one, dbias_one, dgain_two, dbias_two])
    return (dafter + dhidden_norm, grad_rows, grad_fc2, gain_grad)


def segment_kinds(rank_here, cols_here, misc_here):
    column = rank_here * cols_here + jnp.arange(cols_here)
    column_kind = (column >= 3 * D).astype(jnp.int32) + (column >= 4 * D).astype(jnp.int32)
    flat_index = rank_here * misc_here + jnp.arange(misc_here)
    misc_kind = jnp.zeros((misc_here,), jnp.int32)
    offset = 0
    for length in misc_bounds()[:-1]:
        offset += length
        misc_kind = misc_kind + (flat_index >= offset).astype(jnp.int32)
    return (column_kind, misc_kind)


def squares(kinds, rows, fc2, misc, gain_flat):
    column_kind, misc_kind = kinds
    column_sums = jnp.sum(rows * rows, axis=2)
    rows_part = jnp.stack(
        [
            jnp.sum(jnp.where(column_kind == segment, column_sums, 0.0), axis=1)
            for segment in range(3)
        ],
        axis=1,
    ).reshape(-1)
    fc2_part = jnp.sum(fc2 * fc2, axis=(1, 2))
    misc_part = jnp.stack(
        [jnp.sum(jnp.where(misc_kind == segment, misc * misc, 0.0)) for segment in range(6)]
    )
    return jnp.concatenate([rows_part, fc2_part, misc_part, jnp.sum(gain_flat * gain_flat)[None]])


def spread(ratios, kinds, blocks):
    column_kind, misc_kind = kinds
    rows_map = ratios[3 * jnp.arange(blocks)[:, None, None] + column_kind[None, :, None]]
    fc2_map = ratios[3 * blocks + jnp.arange(blocks)][:, None, None]
    misc_map = ratios[4 * blocks + misc_kind]
    return (rows_map, fc2_map, misc_map, ratios[4 * blocks + 6])


def adam_move(grad, weight, first, second, factor, count, decay_now):
    clipped = factor * grad
    first_new = beta_first * first + (1.0 - beta_first) * clipped
    second_new = beta_second * second + (1.0 - beta_second) * clipped * clipped
    first_hat = first_new / (1.0 - beta_first**count)
    second_hat = second_new / (1.0 - beta_second**count)
    return (
        first_new,
        second_new,
        first_hat / (jnp.sqrt(second_hat) + adam_eps) + decay_now * weight,
    )


def plain_local(
    latents,
    noise,
    lengths,
    timesteps,
    labels,
    enc_feats,
    pair_idx,
    step,
    rows_w,
    fc2_w,
    misc_w,
    gains,
    rows_m,
    rows_v,
    fc2_m,
    fc2_v,
    misc_m,
    misc_v,
    gains_m,
    gains_v,
):
    rank_here = lax.axis_index(("dp", "fsdp"))
    count_items = latents.shape[0]
    total_items = count_items * lax.axis_size(("dp", "fsdp"))
    rows_all, fc2_all, misc_all, gains_all = (
        lax.all_gather(rows_w.astype(jnp.bfloat16), ("dp", "fsdp"), axis=1, tiled=True),
        lax.all_gather(fc2_w.astype(jnp.bfloat16), ("dp", "fsdp"), axis=1, tiled=True),
        lax.all_gather(misc_w.astype(jnp.bfloat16), ("dp", "fsdp"), axis=0, tiled=True),
        lax.all_gather(gains.astype(jnp.bfloat16), ("dp", "fsdp"), axis=0, tiled=True),
    )
    embed, head, posit, table, skip, align = split_misc(misc_all)
    gain_rows = gains_all.astype(jnp.float32).reshape(-1, D)
    keymask = jnp.arange(L)[None, :] < lengths[:, None] + 2
    valid = (jnp.arange(PATCH)[None, :] < lengths[:, None]).astype(jnp.float32)
    live_count = lengths.astype(jnp.float32)
    patches = jnp.dot(latents, embed[:PIN], preferred_element_type=jnp.float32) + embed[PIN].astype(
        jnp.float32
    )
    class_rows = jnp.take(table, labels, axis=0).astype(jnp.float32)
    hidden = jnp.concatenate([time_embed(timesteps)[:, None], class_rows[:, None], patches], axis=1)
    hidden = hidden + posit.astype(jnp.float32)[None]
    saved_all = []
    outputs = []
    for block_id in range(BLOCKS):
        if block_id == BLOCKS - 1:
            joined = jnp.concatenate([hidden, outputs[0]], axis=-1).astype(jnp.bfloat16)
            hidden = jnp.dot(joined, skip, preferred_element_type=jnp.float32)
        hidden, saved = block_forward(
            hidden,
            rows_all[block_id],
            fc2_all[block_id],
            gain_rows[4 * block_id : 4 * block_id + 4],
            keymask,
        )
        saved_all.append(saved)
        outputs.append(hidden)
    final, save_final = layer_norm(hidden[:, 2:], gain_rows[12], gain_rows[13])
    final_low = final.astype(jnp.bfloat16)
    pred = jnp.dot(final_low, head, preferred_element_type=jnp.float32)
    denom = live_count * PIN
    diff = (pred - noise) * valid[:, :, None]
    mse_local = jnp.sum(jnp.sum(diff * diff, axis=(1, 2)) / denom) / total_items
    dpred = (2.0 * diff / denom[:, None, None] / total_items).astype(jnp.bfloat16)
    grad_head = collected_sample_embeddings(final_low, dpred)
    dfinal, dgain_final, dbias_final = norm_back(
        gram_crossing(dpred, head), save_final, gain_rows[12]
    )
    middle = outputs[1]
    pooled_low = (jnp.sum(middle[:, 2:] * valid[:, :, None], axis=1) / live_count[:, None]).astype(
        jnp.bfloat16
    )
    projected = jnp.dot(pooled_low, align, preferred_element_type=jnp.float32)
    inverse = lax.rsqrt(jnp.sum(projected * projected, axis=-1, keepdims=True) + vector_eps)
    zhat = projected * inverse
    whole_embedding_table = lax.all_gather(
        zhat.astype(jnp.bfloat16), ("dp", "fsdp"), axis=0, tiled=True
    )
    normalised_latent_embeddings = (
        enc_feats * lax.rsqrt(jnp.sum(enc_feats * enc_feats, axis=-1, keepdims=True) + vector_eps)
    ).astype(jnp.bfloat16)
    cosine_score_table = (
        gram_crossing(normalised_latent_embeddings, whole_embedding_table) / logit_softening_scale
    )
    highest = jnp.max(cosine_score_table, axis=-1, keepdims=True)
    logsum = highest + jnp.log(
        jnp.sum(jnp.exp(cosine_score_table - highest), axis=-1, keepdims=True)
    )
    target = (jnp.arange(total_items)[None, :] == pair_idx[:, None]).astype(jnp.float32)
    align_local = (
        jnp.sum(logsum[:, 0] - jnp.sum(target * cosine_score_table, axis=-1)) / total_items
    )
    cosine_score_derivative = (
        (jnp.exp(cosine_score_table - logsum) - target) * (align_weight / total_items)
    ).astype(jnp.bfloat16)
    feature_set_gradient = (
        collected_sample_embeddings(cosine_score_derivative, normalised_latent_embeddings)
        / logit_softening_scale
    )
    dzhat = lax.psum_scatter(feature_set_gradient, ("dp", "fsdp"), scatter_dimension=0, tiled=True)
    dproj = (inverse * (dzhat - zhat * jnp.sum(dzhat * zhat, axis=-1, keepdims=True))).astype(
        jnp.bfloat16
    )
    grad_align = collected_sample_embeddings(pooled_low, dproj)
    dpooled = gram_crossing(dproj, align)
    dmid_extra = jnp.concatenate(
        [
            jnp.zeros((count_items, 2, D), jnp.float32),
            valid[:, :, None] * dpooled[:, None, :] / live_count[:, None, None],
        ],
        axis=1,
    )
    dhidden = jnp.concatenate([jnp.zeros((count_items, 2, D), jnp.float32), dfinal], axis=1)
    rows_grads = [None] * BLOCKS
    fc2_grads = [None] * BLOCKS
    gain_grads = [None] * BLOCKS
    first_rows_full = None
    first_fc2_full = None
    dshort = None
    grad_skip = None
    for block_id in range(BLOCKS - 1, -1, -1):
        rows_now, fc2_now = (rows_all[block_id], fc2_all[block_id])
        dhidden, grad_rows_full, grad_fc2_full, gain_grads[block_id] = block_backward(
            dhidden,
            rows_now,
            fc2_now,
            gain_rows[4 * block_id : 4 * block_id + 4],
            keymask,
            saved_all[block_id],
        )
        if block_id > 0:
            rows_grads[block_id], fc2_grads[block_id] = (
                lax.psum_scatter(grad_rows_full, ("dp", "fsdp"), scatter_dimension=0, tiled=True),
                lax.psum_scatter(grad_fc2_full, ("dp", "fsdp"), scatter_dimension=0, tiled=True),
            )
        else:
            first_rows_full, first_fc2_full = (grad_rows_full, grad_fc2_full)
        if block_id == BLOCKS - 1:
            dlow = dhidden.astype(jnp.bfloat16)
            grad_skip = collected_sample_embeddings(joined, dlow)
            djoined = gram_crossing(dlow, skip)
            dhidden = djoined[..., :D] + dmid_extra
            dshort = djoined[..., D:]
        elif block_id == 1:
            dhidden = dhidden + dshort
    dpatch = dhidden[:, 2:]
    grad_embed = collected_sample_embeddings(latents, dpatch.astype(jnp.bfloat16))
    grad_patch_bias = jnp.sum(dpatch.reshape(-1, D), axis=0)
    grad_pos = jnp.sum(dhidden, axis=0)
    onehot = (labels[:, None] == jnp.arange(CLS)[None, :]).astype(jnp.float32)
    grad_table = jnp.dot(
        onehot.T, dhidden[:, 1], precision=lax.Precision.HIGHEST, preferred_element_type=jnp.float32
    )
    misc_grad = jnp.concatenate(
        [
            grad_embed.reshape(-1),
            grad_patch_bias,
            grad_head.reshape(-1),
            grad_pos.reshape(-1),
            grad_table.reshape(-1),
            grad_skip.reshape(-1),
            grad_align.reshape(-1),
        ]
    )
    gains_grad = jnp.concatenate(
        [gain_grads[0], gain_grads[1], gain_grads[2], jnp.stack([dgain_final, dbias_final])], axis=0
    ).reshape(-1)
    rows_grads[0], fc2_grads[0], misc_shard, gains_shard = (
        lax.psum_scatter(first_rows_full, ("dp", "fsdp"), scatter_dimension=0, tiled=True),
        lax.psum_scatter(first_fc2_full, ("dp", "fsdp"), scatter_dimension=0, tiled=True),
        lax.psum_scatter(misc_grad, ("dp", "fsdp"), scatter_dimension=0, tiled=True),
        lax.psum_scatter(gains_grad, ("dp", "fsdp"), scatter_dimension=0, tiled=True),
    )
    grads = (jnp.stack(rows_grads), jnp.stack(fc2_grads), misc_shard, gains_shard)
    weights = (rows_w, fc2_w, misc_w, gains)
    firsts = (rows_m, fc2_m, misc_m, gains_m)
    seconds = (rows_v, fc2_v, misc_v, gains_v)
    kinds = segment_kinds(rank_here, rows_w.shape[1], misc_w.shape[0])
    grad_squares, weight_squares, loss = lax.psum(
        (
            squares(kinds, grads[0], grads[1], grads[2], grads[3]),
            squares(kinds, rows_w, fc2_w, misc_w, gains),
            mse_local + align_weight * align_local,
        ),
        ("dp", "fsdp"),
    )
    grad_norm = jnp.sqrt(jnp.sum(grad_squares))
    factor = jnp.minimum(1.0, clip_limit / grad_norm)
    count = step[0].astype(jnp.float32)
    moved = [
        adam_move(
            grads[member],
            weights[member],
            firsts[member],
            seconds[member],
            factor,
            count,
            weight_decay if member < 3 else 0.0,
        )
        for member in range(4)
    ]
    updates = [entry[2] for entry in moved]
    update_squares = lax.psum(
        squares(kinds, updates[0], updates[1], updates[2], updates[3]), ("dp", "fsdp")
    )
    ratios = jnp.sqrt(weight_squares) / jnp.sqrt(update_squares + vector_eps)
    ratio_maps = spread(ratios, kinds, BLOCKS)
    renewed = [
        weights[member] - learn_rate * ratio_maps[member] * updates[member] for member in range(4)
    ]
    norms = jnp.stack([jnp.sqrt(weight_squares), jnp.sqrt(update_squares)], axis=1)
    return (
        loss,
        grad_norm,
        renewed[0],
        moved[0][0],
        moved[0][1],
        renewed[0].astype(jnp.bfloat16),
        renewed[1],
        moved[1][0],
        moved[1][1],
        renewed[1].astype(jnp.bfloat16),
        renewed[2],
        moved[2][0],
        moved[2][1],
        renewed[2].astype(jnp.bfloat16),
        renewed[3],
        moved[3][0],
        moved[3][1],
        renewed[3].astype(jnp.bfloat16),
        norms,
    )


AXES = ("dp", "fsdp")
MESH = pl.DeviceIdType.MESH
LATE = 14
MISC_ROWS = 144
MISC_LATE = PIN + 1 + PIN + L
SKIP_ROW = MISC_LATE + CLS
ALIGN_ROW = SKIP_ROW + 2 * D


def tree_fits(mesh):
    layers, inner = mesh.shape["dp"], mesh.shape["fsdp"]
    devices = layers * inner
    rows = 8 * D // devices
    return inner == 8 and layers == 4 and rows % 16 == 0 and (4 * D) % (inner * rows) == 0


def swap(value, bit):
    count = lax.axis_size(AXES)
    return lax.ppermute(value, AXES, [(i, i ^ bit) for i in range(count)])


def shift_layers(value, step, targets=None):
    layers, inner = lax.axis_size("dp"), lax.axis_size("fsdp")
    pairs = []
    for i in range(layers * inner):
        layer = (i // inner + step) % layers
        if targets is None or layer in targets:
            pairs.append((i, layer * inner + i % inner))
    return lax.ppermute(value, AXES, pairs)


def butterfly_sum(value):
    bit = 1
    while bit < lax.axis_size(AXES):
        value = value + swap(value, bit)
        bit *= 2
    return value


def small_gather(value):
    rank = lax.axis_index(AXES)
    held = value[None]
    bit = 1
    while bit < lax.axis_size(AXES):
        other = swap(held, bit)
        low = (rank // bit) % 2 == 0
        held = jnp.where(
            low, jnp.concatenate([held, other], axis=0), jnp.concatenate([other, held], axis=0)
        )
        bit *= 2
    return held


def gather_kernel(units, n_in, *refs):
    ins = refs[:n_in]
    outs = refs[n_in:2*n_in]
    own, own_sem, store_sem, send_sem, recv_sem = refs[2*n_in:]
    layers = lax.axis_size("dp")
    z, inner = lax.axis_index("dp"), lax.axis_index("fsdp")
    c, x, y = lax.rem(inner, 2), lax.rem(inner // 2, 2), inner // 4
    me = z * 8 + inner
    cross = {"c": inner + 1 - 2 * c, "x": inner + 2 - 4 * x, "y": inner + 4 - 8 * y}

    barrier = pltpu.get_barrier_semaphore()
    for way in "cxy":
        pl.semaphore_signal(barrier, inc=1, device_id=(z, cross[way]), device_id_type=MESH)
    @pl.when(z > 0)
    def _():
        pl.semaphore_signal(barrier, inc=1, device_id=(z - 1, inner), device_id_type=MESH)
    @pl.when(z < layers - 1)
    def _():
        pl.semaphore_signal(barrier, inc=1, device_id=(z + 1, inner), device_id_type=MESH)

    def load(u):
        i, lead, row, rows, _, _ = units[u]
        return pltpu.make_async_copy(ins[i].at[lead, pl.ds(row, rows)], own.at[u, pl.ds(0, rows)], own_sem.at[u])
    def slot(u, d):
        i, lead, row, rows, _, _ = units[u]
        return outs[i].at[lead, d, pl.ds(row, rows)]
    def store(u):
        rows = units[u][3]
        return pltpu.make_async_copy(own.at[u, pl.ds(0, rows)], slot(u, me), store_sem.at[u])
    for u in range(len(units)): load(u).start()
    pl.semaphore_wait(barrier, 3 + (z > 0).astype(jnp.int32) + (z < layers - 1).astype(jnp.int32))

    sends = []
    counts = [0] * len(units)
    def remote(u, d, target, number, from_own=False):
        rows = units[u][3]
        src = own.at[u, pl.ds(0, rows)] if from_own else slot(u, d)
        return pltpu.make_async_remote_copy(src_ref=src, dst_ref=slot(u, d), send_sem=send_sem.at[u, number], recv_sem=recv_sem.at[u, d], device_id=target, device_id_type=MESH)
    def send(u, d, target, cond=None, from_own=False):
        n = counts[u]; counts[u] += 1
        sends.append((u, d, target, n, cond, from_own))
        if cond is None: remote(u, d, target, n, from_own).start()
        else:
            @pl.when(cond)
            def _(): remote(u, d, target, n, from_own).start()
    def arrive(u, d, cond=None):
        if cond is None: remote(u, d, (z, cross["c"]), 0).wait_recv()
        else:
            @pl.when(cond)
            def _(): remote(u, d, (z, cross["c"]), 0).wait_recv()
    up, down = (z + 1, inner), (z - 1, inner)
    def side(way): return (z, cross[way])

    def z_first(u):
        first, second = units[u][5]
        steps = []
        def begin():
            load(u).wait(); store(u).start()
            send(u, me, up, z < layers - 1, True)
            send(u, me, down, z > 0, True)
            for w in (first, second): send(u, me, side(w), None, True)
            send(u, me, side("c"), None, True)
        steps.append(begin)
        def from_z(k, below):
            d = me - 8 * k if below else me + 8 * k
            ok = (z >= k) if below else (z < layers - k)
            def f():
                arrive(u, d, ok)
                if below: send(u, d, up, ok & (z < layers - 1))
                else: send(u, d, down, ok & (z > 0))
                for w in (first, second): send(u, d, side(w), ok)
                send(u, d, side("c"), ok)
            return f
        for k in range(1, layers):
            steps.append(from_z(k, True)); steps.append(from_z(k, False))
        def from_side(k, below):
            dz = 0 if k == 0 else (-8 * k if below else 8 * k)
            ok = None if k == 0 else ((z >= k) if below else (z < layers - k))
            def f():
                d = z * 8 + dz + cross[first]
                arrive(u, d, ok)
                send(u, d, side(second), ok)
                send(u, d, side("c"), ok)
                d2 = z * 8 + dz + cross[second]
                arrive(u, d2, ok)
                send(u, d2, side("c"), ok)
            return f
        def from_far(k, below):
            dz = 0 if k == 0 else (-8 * k if below else 8 * k)
            ok = None if k == 0 else ((z >= k) if below else (z < layers - k))
            def f():
                d = z * 8 + dz + cross["x"] + cross["y"] - inner
                arrive(u, d, ok)
                send(u, d, side("c"), ok)
            return f
        order = [(0, True)] + [(k, b) for k in range(1, layers) for b in (True, False)]
        for kb in order: steps.append(from_side(*kb))
        for kb in order: steps.append(from_far(*kb))
        return steps
    def z_last(u):
        first, second = units[u][5]
        steps = []
        def begin():
            load(u).wait(); store(u).start()
            for w in (first, second): send(u, me, side(w), None, True)
            send(u, me, up, z < layers - 1, True)
            send(u, me, down, z > 0, True)
            send(u, me, side("c"), None, True)
        steps.append(begin)
        far = cross["x"] + cross["y"] - inner
        def spread(d):
            send(u, d, up, z < layers - 1)
            send(u, d, down, z > 0)
            send(u, d, side("c"))
        def f1():
            d = z * 8 + cross[first]; arrive(u, d); send(u, d, side(second)); spread(d)
            d = z * 8 + cross[second]; arrive(u, d); spread(d)
        def f2():
            d = z * 8 + far; arrive(u, d); spread(d)
        steps += [f1, f2]
        def from_z(k, below):
            ok = (z >= k) if below else (z < layers - k)
            def f():
                for col in (inner, cross[first], cross[second], far):
                    d = (z - k if below else z + k) * 8 + col
                    arrive(u, d, ok)
                    if below: send(u, d, up, ok & (z < layers - 1))
                    else: send(u, d, down, ok & (z > 0))
                    send(u, d, side("c"), ok)
            return f
        for k in range(1, layers):
            steps.append(from_z(k, True)); steps.append(from_z(k, False))
        return steps
    plans = [z_first(u) if units[u][4] == "z" else z_last(u) for u in range(len(units))]
    agenda = sorted(
        ((s if units[u][4] == "z" or s < 3 else LATE + s - 3) + u, u, s)
        for u in range(len(units))
        for s in range(len(plans[u]))
    )
    for _, u, s in agenda: plans[u][s]()
    for u in range(len(units)):
        for d in range(layers * 4):
            arrive(u, 2 * d + 1 - c)
        store(u).wait()
    for u, d, target, n, cond, from_own in sends:
        if cond is None: remote(u, d, target, n, from_own).wait_send()
        else:
            @pl.when(cond)
            def _(u=u, d=d, target=target, n=n, from_own=from_own): remote(u, d, target, n, from_own).wait_send()

def gather_all(units, arrays, cid=0):
    devices = lax.axis_size(("dp","fsdp"))
    U = len(units)
    rows = max(u[3] for u in units)
    width = arrays[0].shape[-1]
    return pl.pallas_call(
        functools.partial(gather_kernel, units, len(arrays)),
        out_shape=[jax.ShapeDtypeStruct((a.shape[0], devices) + a.shape[1:], a.dtype) for a in arrays],
        in_specs=[pl.BlockSpec(memory_space=pl.ANY)] * len(arrays),
        out_specs=[pl.BlockSpec(memory_space=pl.ANY)] * len(arrays),
        scratch_shapes=[pltpu.VMEM((U, rows, width), jnp.bfloat16), pltpu.SemaphoreType.DMA((U,)), pltpu.SemaphoreType.DMA((U,)),
            pltpu.SemaphoreType.DMA((U, 64)), pltpu.SemaphoreType.DMA((U, devices))],
        compiler_params=pltpu.CompilerParams(collective_id=cid, has_side_effects=True, vmem_limit_bytes=16<<20),
        name="gather_all")(*arrays)


def gather_weights(rows, fc2, misc):
    rows_each, half = rows.shape[1], rows.shape[1] // 2
    ways = (("x", "y"), ("y", "x"))
    units = [(2, 0, 0, misc.shape[1], "last", ways[0]), (1, 0, 0, fc2.shape[1], "last", ways[1])]
    for block_id in range(BLOCKS):
        units += [(0, block_id, row, half, "z", ways[row // half]) for row in (0, half)]
        if block_id > 0:
            units.append((1, block_id, 0, fc2.shape[1], "z", ways[block_id % 2]))
    return gather_all(units, [rows, fc2, misc])


def greet(partners):
    barrier = pltpu.get_barrier_semaphore()
    for partner in partners:
        pl.semaphore_signal(barrier, inc=1, device_id=partner, device_id_type=MESH)
    pl.semaphore_wait(barrier, len(partners))


def owner_sum_kernel(groups, *refs):
    n = len(groups)
    ys, xs = refs[:n], refs[n : 2 * n]
    outs = refs[2 * n : 3 * n]
    scratch = refs[3 * n :]
    names = ("y_own", "y_far", "x_far", "part", "got_one", "got_two", "got_z",
             "load_sem", "ex_send", "ex_recv", "x_sem", "part_send", "one_recv", "two_recv", "z_send", "z_recv")
    per = len(names)
    layers = lax.axis_size("dp")
    z, inner = lax.axis_index("dp"), lax.axis_index("fsdp")
    c, x, y = lax.rem(inner, 2), lax.rem(inner // 2, 2), inner // 4
    other = (z, inner + 1 - 2 * c)
    sides = ((z, inner + 2 - 4 * x), (z, inner + 4 - 8 * y))
    columns = [(lax.rem(z + k, layers), inner) for k in range(1, layers)]

    def chip_of(group, slot):
        b, a = lax.rem(slot // 2, 2), lax.rem(slot, 2)
        yy, xx = y + b - 2 * y * b, x + a - 2 * x * a
        return (slot // 4) * 4 + yy * 2 + xx

    parts = []
    for g, group in enumerate(groups):
        s = dict(zip(names, scratch[g * per : (g + 1) * per]))
        s.update(y=ys[g], x=xs[g], x_own=xs[g], out=outs[g], group=group, slots=4 * group[1])
        parts.append(s)

    def x_there(s):
        return pltpu.make_async_remote_copy(
            src_ref=s["x"], dst_ref=s["x_far"], send_sem=s["x_sem"].at[0], recv_sem=s["x_sem"].at[1],
            device_id=other, device_id_type=MESH)

    def y_here(s, slot):
        return pltpu.make_async_copy(s["y"].at[chip_of(s["group"], slot), c], s["y_own"].at[slot], s["load_sem"].at[slot])

    def y_there(s, slot):
        return pltpu.make_async_remote_copy(
            src_ref=s["y"].at[chip_of(s["group"], slot), 1 - c], dst_ref=s["y_far"].at[slot],
            send_sem=s["ex_send"].at[slot], recv_sem=s["ex_recv"].at[slot], device_id=other, device_id_type=MESH)

    def slot_of(kind, layer, first, second):
        return layer * 4 + (second * 2 + first if kind == 0 else first * 2 + second)

    def one_there(s, kind, layer, second):
        return pltpu.make_async_remote_copy(
            src_ref=s["part"].at[slot_of(kind, layer, 1, second)], dst_ref=s["got_one"].at[layer * 2 + second],
            send_sem=s["part_send"].at[slot_of(kind, layer, 1, second)], recv_sem=s["one_recv"].at[layer * 2 + second],
            device_id=sides[kind], device_id_type=MESH)

    def two_there(s, kind, layer):
        return pltpu.make_async_remote_copy(
            src_ref=s["part"].at[slot_of(kind, layer, 0, 1)], dst_ref=s["got_two"].at[layer],
            send_sem=s["part_send"].at[slot_of(kind, layer, 0, 1)], recv_sem=s["two_recv"].at[layer],
            device_id=sides[1 - kind], device_id_type=MESH)

    def z_there(s, kind, layer):
        target = s["group"][0] + layer
        hop = lax.rem(target - z + layers, layers)
        spot = jnp.maximum(hop - 1, 0)
        return pltpu.make_async_remote_copy(
            src_ref=s["part"].at[slot_of(kind, layer, 0, 0)], dst_ref=s["got_z"].at[spot],
            send_sem=s["z_send"].at[layer], recv_sem=s["z_recv"].at[spot],
            device_id=(target, inner), device_id_type=MESH)

    def product(s, slot):
        y_here(s, slot).wait()
        y_there(s, slot).wait_recv()
        if s["group"][2] > 1:
            rows = s["out"].shape[0]
            owner = (s["group"][0] * 4 + chip_of(s["group"], slot)) * 2 + c
            kind = (owner * rows >= s["group"][3]).astype(jnp.int32)
        else:
            kind = 0
        return jnp.dot(s["y_own"][slot], s["x_own"][kind], preferred_element_type=jnp.float32) + jnp.dot(
            s["y_far"][slot], s["x_far"][kind], preferred_element_type=jnp.float32)

    greet([other, *sides, *columns])
    for s in parts:
        x_there(s).start()
        @pl.loop(0, s["slots"])
        def _(i):
            y_there(s, i).start()
    for s in parts:
        half = (s["group"][1] + 1) // 2
        s["kinds"] = [(0, 0, half), (1, half, s["group"][1])]
    def first_step(s):
        x_there(s).wait_recv()
        for kind, lo, hi in s["kinds"]:
            for second in (1, 0):
                @pl.loop(lo, hi)
                def _(layer):
                    slot = slot_of(kind, layer, 1, second)
                    s["part"][slot] = product(s, slot).astype(jnp.bfloat16)
                    one_there(s, kind, layer, second).start()
    def second_step(s):
        for kind, lo, hi in s["kinds"]:
            @pl.loop(lo, hi)
            def _(layer):
                slot = slot_of(kind, layer, 0, 1)
                own = product(s, slot)
                one_there(s, kind, layer, 1).wait_recv()
                s["part"][slot] = (own + s["got_one"][layer * 2 + 1].astype(jnp.float32)).astype(jnp.bfloat16)
                two_there(s, kind, layer).start()
    def third_step(s):
        for kind, lo, hi in s["kinds"]:
            @pl.loop(lo, hi)
            def _(layer):
                slot = slot_of(kind, layer, 0, 0)
                own = product(s, slot)
                one_there(s, kind, layer, 0).wait_recv()
                two_there(s, kind, layer).wait_recv()
                total = own + s["got_one"][layer * 2].astype(jnp.float32) + s["got_two"][layer].astype(jnp.float32)
                s["part"][slot] = total.astype(jnp.bfloat16)
                @pl.when(s["group"][0] + layer != z)
                def _():
                    z_there(s, kind, layer).start()
    def last_step(s):
        lo, count = s["group"][:2]
        inside = (z >= lo) & (z < lo + count)
        for kind, a, b in s["kinds"]:
            @pl.loop(a, b)
            def _(layer):
                @pl.when(lo + layer == z)
                def _():
                    total = s["part"][slot_of(kind, layer, 0, 0)].astype(jnp.float32)
                    for k in range(layers - 1):
                        pltpu.make_async_remote_copy(
                            src_ref=s["got_z"].at[k], dst_ref=s["got_z"].at[k], send_sem=s["z_send"].at[0],
                            recv_sem=s["z_recv"].at[k], device_id=columns[0], device_id_type=MESH).wait_recv()
                        total = total + s["got_z"][k].astype(jnp.float32)
                    s["out"][...] = total
        if count < layers:
            @pl.when(jnp.logical_not(inside))
            def _():
                s["out"][...] = jnp.zeros_like(s["out"])
    for s in parts:
        @pl.loop(0, s["slots"])
        def _(i):
            y_here(s, i).start()
    for s in parts:
        first_step(s)
    for s in parts:
        second_step(s)
    for s in parts:
        third_step(s)
    for s in parts:
        last_step(s)
    for s in parts:
        x_there(s).wait_send()
        @pl.loop(0, s["slots"])
        def _(i):
            y_there(s, i).wait_send()
        for kind, lo, hi in s["kinds"]:
            @pl.loop(lo, hi)
            def _(layer):
                for second in (0, 1):
                    one_there(s, kind, layer, second).wait_send()
                two_there(s, kind, layer).wait_send()
                @pl.when(s["group"][0] + layer != z)
                def _():
                    z_there(s, kind, layer).wait_send()


def owner_sums(groups, ys, xs, cid):
    scratch = []
    shapes = []
    layers = lax.axis_size("dp")
    for group, y, x in zip(groups, ys, xs):
        count, (rows, tokens) = group[1], y.shape[2:]
        slots = 4 * count
        dma = pltpu.SemaphoreType.DMA
        low = jnp.bfloat16
        scratch += [
            pltpu.VMEM((slots, rows, tokens), low),
            pltpu.VMEM((slots, rows, tokens), low),
            pltpu.VMEM(x.shape, low),
            pltpu.VMEM((slots, rows, D), low),
            pltpu.VMEM((2 * count, rows, D), low),
            pltpu.VMEM((count, rows, D), low),
            pltpu.VMEM((layers - 1, rows, D), low),
            dma((slots,)), dma((slots,)), dma((slots,)), dma((2,)), dma((slots,)), dma((2 * count,)), dma((count,)), dma((count,)), dma((layers - 1,)),
        ]
        shapes.append(jax.ShapeDtypeStruct((rows, D), jnp.float32))
    return pl.pallas_call(
        functools.partial(owner_sum_kernel, groups),
        out_shape=shapes,
        in_specs=[pl.BlockSpec(memory_space=pl.ANY)] * len(ys) + [pl.BlockSpec(memory_space=pltpu.VMEM)] * len(xs),
        out_specs=[pl.BlockSpec(memory_space=pltpu.VMEM)] * len(ys),
        scratch_shapes=scratch,
        compiler_params=pltpu.CompilerParams(collective_id=cid, has_side_effects=True, vmem_limit_bytes=60 << 20),
        name="owner_sums",
    )(*ys, *xs)


def product_kernel(table, y_own, y_other, x_own, x_other, out):
    out[0] = (
        jnp.dot(y_own[0], x_own[0], preferred_element_type=jnp.float32)
        + jnp.dot(y_other[0], x_other[0], preferred_element_type=jnp.float32)
    ).astype(jnp.bfloat16)


def products(table, count, y_own, y_other, x_own, x_other):
    rows, tokens = y_own.shape[1:]
    width = x_own.shape[-1]
    return pl.pallas_call(
        product_kernel,
        out_shape=jax.ShapeDtypeStruct((count, rows, width), jnp.bfloat16),
        grid_spec=pltpu.PrefetchScalarGridSpec(
            num_scalar_prefetch=1,
            grid=(count,),
            in_specs=[
                pl.BlockSpec((1, rows, tokens), lambda n, t: (t[n], 0, 0)),
                pl.BlockSpec((1, rows, tokens), lambda n, t: (t[count + n], 0, 0)),
                pl.BlockSpec((1, tokens, width), lambda n, t: (t[2 * count + n], 0, 0)),
                pl.BlockSpec((1, tokens, width), lambda n, t: (t[2 * count + n], 0, 0)),
            ],
            out_specs=pl.BlockSpec((1, rows, width), lambda n, t: (n, 0, 0)),
        ),
        compiler_params=pltpu.CompilerParams(vmem_limit_bytes=24 << 20),
        cost_estimate=pl.CostEstimate(
            flops=4 * count * rows * tokens * width,
            bytes_accessed=2 * count * rows * (width + 2 * tokens),
            transcendentals=0,
        ),
        name="products",
    )(table, y_own, y_other, x_own, x_other)


def add_low(*terms):
    total = terms[0].astype(jnp.float32)
    for term in terms[1:]:
        total = total + term.astype(jnp.float32)
    return total.astype(jnp.bfloat16)


def scatter_products(y_parts, x_parts, layers_here, kind_of):
    inner = lax.axis_index("fsdp")
    core, x_bit, y_bit = inner % 2, (inner // 2) % 2, inner // 4
    count_layers = len(layers_here)
    rows, tokens = y_parts.shape[1:]
    by_core = y_parts.reshape(count_layers * 4, 2, rows, tokens)
    sent = lax.dynamic_index_in_dim(by_core, 1 - core, axis=1, keepdims=False)
    y_other = swap(sent, 1)
    x_other = swap(x_parts, 1)
    half = (count_layers + 1) // 2

    def table_of(spots):
        own, other, kinds = [], [], []
        for place, flip_x, flip_y in spots:
            chip = place * 4 + (y_bit ^ flip_y) * 2 + (x_bit ^ flip_x)
            own.append(2 * chip + core)
            other.append(chip)
            kinds.append(kind_of(layers_here[0] * 8 + 2 * chip + core))
        return jnp.stack(own + other + kinds).astype(jnp.int32)

    def make(spots, lead):
        made = products(table_of(spots), len(spots), y_parts, y_other, x_parts, x_other)
        return made.reshape(lead + (rows, D))

    halves = []
    for which, places in enumerate((range(half), range(half, count_layers))):
        if len(places) == 0:
            continue
        n = len(places)
        first, second = ((2, 4), (4, 2))[which]
        spots = {}
        for flip_first in (1, 0):
            spots[flip_first] = [
                (p, flip_first, flip_second) if which == 0 else (p, flip_second, flip_first)
                for flip_second in (0, 1)
                for p in places
            ]
        away = swap(make(spots[1], (2, n)), first)
        kept = make(spots[0], (2, n))
        far = swap(add_low(kept[1], away[1]), second)
        halves.append(add_low(kept[0], away[0], far))
    summed = halves[0] if len(halves) == 1 else jnp.concatenate(halves, axis=0)
    return scatter_layers(summed, layers_here)


def scatter_layers(summed, layers_here):
    layer = lax.axis_index("dp")
    layers = lax.axis_size("dp")

    def for_layer(target):
        spot = jnp.clip(target - layers_here[0], 0, len(layers_here) - 1)
        return lax.dynamic_index_in_dim(summed, spot, axis=0, keepdims=False)

    total = for_layer(layer).astype(jnp.float32)
    for k in range(1, layers):
        got = shift_layers(for_layer((layer + k) % layers), k, layers_here)
        total = total + got.astype(jnp.float32)
    return total


def scatter_first_layer(full):
    inner = lax.axis_index("fsdp")
    held = full.astype(jnp.bfloat16).reshape(2, 2, 2, full.shape[1], D)
    for axis, bit in ((2, 1), (1, 2), (0, 4)):
        mine = (inner // bit) % 2
        away = swap(lax.dynamic_index_in_dim(held, 1 - mine, axis=axis, keepdims=False), bit)
        kept = lax.dynamic_index_in_dim(held, mine, axis=axis, keepdims=False)
        held = add_low(kept, away)
    return scatter_layers(held[None], [0])


def dot(left, right, over, batch=((), ())):
    return lax.dot_general(
        left, right, ((over[:1], over[1:]), batch), preferred_element_type=jnp.float32
    )


HEADS = ((0,), (0,))


def masked_scores(queries, keys_all, keymask):
    scores = dot(queries, keys_all, (1, 1), HEADS) * HD ** (-0.5)
    return jnp.where(keymask[None, None, :], scores, mask_fill)


def fast_forward(hidden, weights, fc2, gvec, keymask):
    normed, save_one = layer_norm(hidden, gvec[0], gvec[1])
    normed_low = normed.astype(jnp.bfloat16)
    triple = dot(weights[: 3 * D], normed_low, (1, 1)).astype(jnp.bfloat16).reshape(3, H, HD, L)
    scores = masked_scores(triple[0], triple[1], keymask)
    highest = jnp.max(scores, axis=-1, keepdims=True)
    logsum = highest + jnp.log(jnp.sum(jnp.exp(scores - highest), axis=-1, keepdims=True))
    probs = jnp.exp(scores - logsum).astype(jnp.bfloat16)
    attended = dot(triple[2], probs, (2, 2), HEADS).astype(jnp.bfloat16).reshape(D, L)
    after = hidden + dot(attended, weights[3 * D : 4 * D], (0, 1))
    normed_two, save_two = layer_norm(after, gvec[2], gvec[3])
    normed_two_low = normed_two.astype(jnp.bfloat16)
    inner = dot(weights[4 * D :], normed_two_low, (1, 1))
    active = jax.nn.gelu(inner, approximate=True).astype(jnp.bfloat16)
    output = after + dot(active, fc2, (0, 0))
    return output, (
        save_one,
        normed_low,
        triple,
        logsum,
        attended,
        save_two,
        normed_two_low,
        inner,
        active,
    )


def fast_backward(dout, weights, fc2, gvec, keymask, saved):
    save_one, normed_low, triple, logsum, attended, save_two, normed_two_low, inner, active = saved
    devices = lax.axis_size(AXES)
    layers = lax.axis_size("dp")
    rows_each = 8 * D // devices
    dlow = dout.astype(jnp.bfloat16)
    dactive = dot(fc2, dlow, (1, 1))
    slope = jax.vjp(lambda entry: jax.nn.gelu(entry, approximate=True), inner)[1](dactive)[0]
    dinner = slope.astype(jnp.bfloat16)
    dnormed_two = dot(dinner, weights[4 * D :], (0, 0))
    dafter_norm, dgain_two, dbias_two = norm_back(dnormed_two, save_two, gvec[2])
    dafter = dout + dafter_norm
    dafter_low = dafter.astype(jnp.bfloat16)
    dattended = dot(weights[3 * D : 4 * D], dafter_low, (0, 1)).astype(jnp.bfloat16)
    dattended = dattended.reshape(H, HD, L)
    probs = jnp.exp(masked_scores(triple[0], triple[1], keymask) - logsum)
    dprobs = dot(dattended, triple[2], (1, 1), HEADS)
    dscores = (probs * (dprobs - jnp.sum(probs * dprobs, axis=-1, keepdims=True))).astype(
        jnp.bfloat16
    )
    dqueries = dot(triple[1], dscores, (2, 2), HEADS) * HD ** (-0.5)
    dkeys = dot(triple[0], dscores, (2, 1), HEADS) * HD ** (-0.5)
    dvalues = dot(dattended, probs.astype(jnp.bfloat16), (2, 1), HEADS)
    dtriple = jnp.stack([dqueries, dkeys, dvalues]).astype(jnp.bfloat16).reshape(3 * D, L)
    lower_parts = jnp.concatenate([dtriple, dafter_low.T], axis=0)
    half = layers // 2
    groups = [(0, layers, 1, 0), (half, layers - half, 1, 0), (0, half, 2, 3 * D)]
    grad_fc2, grad_upper, grad_lower = owner_sums(
        groups,
        [
            active.reshape(devices // 2, 2, rows_each // 2, L),
            dinner.reshape(devices // 4, 2, rows_each, L),
            lower_parts.reshape(devices // 4, 2, rows_each, L),
        ],
        [dlow[None], normed_two_low[None], jnp.stack([normed_low, attended.T])],
        1,
    )
    dnormed = dot(dtriple, weights[: 3 * D], (0, 0))
    dhidden_norm, dgain_one, dbias_one = norm_back(dnormed, save_one, gvec[0])
    gain_grad = jnp.stack([dgain_one, dbias_one, dgain_two, dbias_two])
    grad_rows = jnp.where(lax.axis_index("dp") >= half, grad_upper, grad_lower)
    return dafter + dhidden_norm, grad_rows, grad_fc2, gain_grad


def row_starts(devices, misc_here):
    return [(d * misc_here) // D for d in range(devices)]


def misc_rows(pieces, starts, lo, hi):
    total = jnp.zeros((hi - lo, D), pieces.dtype)
    used = MISC_ROWS - 4
    for d, start in enumerate(starts):
        first, last = max(start, lo), min(start + used, hi)
        if first < last:
            part = pieces[d, first - start : last - start]
            total = total + jnp.pad(part, ((first - lo, hi - last), (0, 0)))
    return total


def fast_local(
    latents,
    noise,
    lengths,
    timesteps,
    labels,
    enc_feats,
    pair_idx,
    step,
    rows_w,
    fc2_w,
    misc_w,
    gains,
    rows_m,
    rows_v,
    fc2_m,
    fc2_v,
    misc_m,
    misc_v,
    gains_m,
    gains_v,
):
    rank_here = lax.axis_index(AXES)
    total_items = devices = lax.axis_size(AXES)
    layers = lax.axis_size("dp")
    misc_here, gains_here = misc_w.shape[0], gains.shape[0]
    starts = row_starts(devices, misc_here)
    start_here = (rank_here * misc_here) // D
    offset_here = rank_here * misc_here - start_here * D

    encoded = (
        enc_feats * lax.rsqrt(jnp.sum(enc_feats * enc_feats, axis=-1, keepdims=True) + vector_eps)
    ).astype(jnp.bfloat16)
    used = MISC_ROWS - 4
    flat = lax.dynamic_update_slice(
        jnp.zeros((used * D,), jnp.bfloat16), misc_w.astype(jnp.bfloat16), (offset_here,)
    )
    extra = jnp.stack(
        [
            jnp.pad(gains.astype(jnp.bfloat16), (0, D - gains_here)),
            jnp.pad(encoded[0], (0, D - ENC)),
            jnp.pad(pair_idx.astype(jnp.bfloat16), (0, D - 1)),
            jnp.zeros((D,), jnp.bfloat16),
        ]
    )
    piece_misc = jnp.concatenate([flat.reshape(used, D), extra], axis=0)
    rows_full, fc2_full, misc_full = gather_weights(
        rows_w.astype(jnp.bfloat16), fc2_w.astype(jnp.bfloat16), piece_misc[None]
    )
    pieces = misc_full[0]
    rows_all = [rows_full[block_id].reshape(8 * D, D) for block_id in range(BLOCKS)]
    fc2_all = [fc2_full[block_id].reshape(4 * D, D) for block_id in range(BLOCKS)]

    gains_all = pieces[:, used, :gains_here].reshape(-1)
    gain_rows = gains_all.astype(jnp.float32).reshape(-1, D)
    encoded_all = pieces[:, used + 1, :ENC]
    pairs_all = pieces[:, used + 2, 0].astype(jnp.int32)
    front = misc_rows(pieces, starts, 0, MISC_LATE)
    embed = front[: PIN + 1]
    head = front[PIN + 1 : 2 * PIN + 1].reshape(D, PIN)
    posit = front[2 * PIN + 1 :].astype(jnp.float32)
    skip = misc_rows(pieces, starts, SKIP_ROW, ALIGN_ROW)
    align = misc_rows(pieces, starts, ALIGN_ROW, ALIGN_ROW + ENC).reshape(D, ENC)
    class_place = MISC_LATE + labels[0]
    owner_first = (class_place * D) // misc_here
    owner_last = (class_place * D + D - 1) // misc_here

    def class_part(owner):
        return lax.dynamic_slice(
            pieces, (owner, class_place - (owner * misc_here) // D, 0), (1, 1, D)
        )[0].astype(jnp.float32)

    class_row = class_part(owner_first) + jnp.where(
        owner_last > owner_first, class_part(owner_last), 0.0
    )

    keymask = jnp.arange(L) < lengths[0] + 2
    valid = (jnp.arange(PATCH) < lengths[0]).astype(jnp.float32)[:, None]
    live_count = lengths[0].astype(jnp.float32)
    patches = jnp.dot(latents[0], embed[:PIN], preferred_element_type=jnp.float32) + embed[
        PIN
    ].astype(jnp.float32)
    tokens = jnp.concatenate([time_embed(timesteps), class_row, patches], axis=0) + posit

    def gvec(block_id):
        return gain_rows[4 * block_id : 4 * block_id + 4]

    shallow, saved_shallow = fast_forward(tokens, rows_all[0], fc2_all[0], gvec(0), keymask)
    middle, saved_middle = fast_forward(shallow, rows_all[1], fc2_all[1], gvec(1), keymask)
    joined = jnp.concatenate([middle, shallow], axis=-1).astype(jnp.bfloat16)
    deep_in = jnp.dot(joined, skip, preferred_element_type=jnp.float32)
    deep, saved_deep = fast_forward(deep_in, rows_all[2], fc2_all[2], gvec(2), keymask)

    pooled = (jnp.sum(middle[2:] * valid, axis=0) / live_count).astype(jnp.bfloat16)
    pooled_all = small_gather(pooled)
    projected = jnp.dot(pooled_all, align, preferred_element_type=jnp.float32)
    inverse = lax.rsqrt(jnp.sum(projected * projected, axis=-1, keepdims=True) + vector_eps)
    zhat = projected * inverse
    logits = gram_crossing(encoded_all, zhat.astype(jnp.bfloat16)) / logit_softening_scale
    highest = jnp.max(logits, axis=-1, keepdims=True)
    logsum = highest + jnp.log(jnp.sum(jnp.exp(logits - highest), axis=-1, keepdims=True))
    target = (jnp.arange(total_items)[None, :] == pairs_all[:, None]).astype(jnp.float32)
    align_loss = jnp.sum(logsum[:, 0] - jnp.sum(target * logits, axis=-1)) / total_items
    dlogits = ((jnp.exp(logits - logsum) - target) * (align_weight / total_items)).astype(
        jnp.bfloat16
    )
    dzhat = collected_sample_embeddings(dlogits, encoded_all) / logit_softening_scale
    dproj = (inverse * (dzhat - zhat * jnp.sum(dzhat * zhat, axis=-1, keepdims=True))).astype(
        jnp.bfloat16
    )
    grad_align = collected_sample_embeddings(pooled_all, dproj).reshape(ENC, D)
    dpooled = gram_crossing(lax.dynamic_slice_in_dim(dproj, rank_here, 1, axis=0), align)
    dmid_extra = jnp.pad(valid * dpooled / live_count, ((2, 0), (0, 0)))

    final, save_final = layer_norm(deep[2:], gain_rows[12], gain_rows[13])
    final_low = final.astype(jnp.bfloat16)
    pred = jnp.dot(final_low, head, preferred_element_type=jnp.float32)
    denom = live_count * PIN
    diff = (pred - noise[0]) * valid
    mse_local = jnp.sum(diff * diff) / denom / total_items
    dpred = (2.0 * diff / denom / total_items).astype(jnp.bfloat16)
    grad_head = collected_sample_embeddings(final_low, dpred)
    dfinal, dgain_final, dbias_final = norm_back(
        gram_crossing(dpred, head), save_final, gain_rows[12]
    )

    rows_grads = [None] * BLOCKS
    fc2_grads = [None] * BLOCKS
    gain_grads = [None] * BLOCKS
    dhidden = jnp.pad(dfinal, ((2, 0), (0, 0)))
    dhidden, rows_grads[2], fc2_grads[2], gain_grads[2] = fast_backward(
        dhidden, rows_all[2], fc2_all[2], gvec(2), keymask, saved_deep
    )
    dlow = dhidden.astype(jnp.bfloat16)
    joined_features = joined.T
    skip_parts = []
    for d in range(devices // layers, devices):
        first = max(starts[d], SKIP_ROW)
        last = min(starts[d] + used, ALIGN_ROW)
        if first < last:
            part = joined_features[first - SKIP_ROW : last - SKIP_ROW]
            part = jnp.pad(
                part, ((first - starts[d], MISC_ROWS - (last - starts[d])), (0, 0))
            )
        else:
            part = jnp.zeros((MISC_ROWS, L), jnp.bfloat16)
        skip_parts.append(part)
    grad_skip = scatter_products(
        jnp.stack(skip_parts), dlow[None], list(range(1, layers)), lambda owner: owner * 0
    )
    djoined = gram_crossing(dlow, skip)
    dhidden = djoined[:, :D] + dmid_extra
    dshort = djoined[:, D:]
    dhidden, rows_grads[1], fc2_grads[1], gain_grads[1] = fast_backward(
        dhidden, rows_all[1], fc2_all[1], gvec(1), keymask, saved_middle
    )
    dhidden = dhidden + dshort
    dhidden, rows_grads[0], fc2_grads[0], gain_grads[0] = fast_backward(
        dhidden, rows_all[0], fc2_all[0], gvec(0), keymask, saved_shallow
    )

    dpatch = dhidden[2:]
    grad_embed = collected_sample_embeddings(latents[0], dpatch.astype(jnp.bfloat16))
    late = jnp.concatenate(
        [
            grad_embed,
            jnp.sum(dpatch, axis=0, keepdims=True),
            grad_head.reshape(PIN, D),
            dhidden,
        ],
        axis=0,
    )
    inner = devices // layers
    late_parts = []
    for d in range(inner):
        first, last = starts[d], min(starts[d] + used, MISC_LATE)
        if first < last:
            late_parts.append(jnp.pad(late[first:last], ((0, MISC_ROWS - (last - first)), (0, 0))))
        else:
            late_parts.append(jnp.zeros((MISC_ROWS, D), jnp.float32))
    grad_late = scatter_first_layer(jnp.stack(late_parts))
    class_grads = small_gather(dhidden[1])
    class_rows = MISC_LATE + small_gather(labels.astype(jnp.float32)).astype(jnp.int32)[:, 0]
    hit = (
        class_rows[None, :] == start_here + jnp.arange(MISC_ROWS)[:, None]
    ).astype(jnp.float32)
    grad_class = jnp.dot(
        hit, class_grads, precision=lax.Precision.HIGHEST, preferred_element_type=jnp.float32
    )
    align_first = starts[-1] + MISC_ROWS
    grad_align = jnp.pad(
        grad_align, ((MISC_ROWS, align_first - (ALIGN_ROW + ENC)), (0, 0))
    )
    align_here = lax.dynamic_slice_in_dim(
        grad_align, jnp.maximum(start_here - (ALIGN_ROW - MISC_ROWS), 0), MISC_ROWS, axis=0
    )
    grad_piece = (
        jnp.where(lax.axis_index("dp") == 0, grad_late, grad_skip) + grad_class + align_here
    )
    misc_shard = lax.dynamic_slice(grad_piece.reshape(-1), (offset_here,), (misc_here,))
    gains_sum = butterfly_sum(
        jnp.concatenate(
            [
                gain_grads[0],
                gain_grads[1],
                gain_grads[2],
                jnp.stack([dgain_final, dbias_final]),
                jnp.zeros((2, D), jnp.float32),
            ],
            axis=0,
        )
    )
    gains_shard = lax.dynamic_slice_in_dim(
        gains_sum.reshape(-1), rank_here * gains_here, gains_here
    )

    grads = (jnp.stack(rows_grads), jnp.stack(fc2_grads), misc_shard, gains_shard)
    weights = (rows_w, fc2_w, misc_w, gains)
    firsts = (rows_m, fc2_m, misc_m, gains_m)
    seconds = (rows_v, fc2_v, misc_v, gains_v)
    kinds = segment_kinds(rank_here, rows_w.shape[1], misc_w.shape[0])
    matrices = 4 * BLOCKS + 7
    sums = butterfly_sum(
        jnp.concatenate(
            [
                squares(kinds, grads[0], grads[1], grads[2], grads[3]),
                squares(kinds, rows_w, fc2_w, misc_w, gains),
                mse_local[None],
            ]
        )
    )
    weight_squares = sums[matrices : 2 * matrices]
    loss = sums[2 * matrices] + align_weight * align_loss
    grad_norm = jnp.sqrt(jnp.sum(sums[:matrices]))
    factor = jnp.minimum(1.0, clip_limit / grad_norm)
    count = step[0].astype(jnp.float32)
    moved = [
        adam_move(
            grads[member],
            weights[member],
            firsts[member],
            seconds[member],
            factor,
            count,
            weight_decay if member < 3 else 0.0,
        )
        for member in range(4)
    ]
    updates = [entry[2] for entry in moved]
    update_squares = butterfly_sum(squares(kinds, updates[0], updates[1], updates[2], updates[3]))
    ratios = jnp.sqrt(weight_squares) / jnp.sqrt(update_squares + vector_eps)
    ratio_maps = spread(ratios, kinds, BLOCKS)
    renewed = [
        weights[member] - learn_rate * ratio_maps[member] * updates[member] for member in range(4)
    ]
    norms = jnp.stack([jnp.sqrt(weight_squares), jnp.sqrt(update_squares)], axis=1)
    outputs = [loss, grad_norm]
    for member in range(4):
        outputs += [
            renewed[member],
            moved[member][0],
            moved[member][1],
            renewed[member].astype(jnp.bfloat16),
        ]
    return tuple(outputs) + (norms,)


def solution(mesh):
    body = fast_local if tree_fits(mesh) else plain_local
    in_specs = (
        P(("dp", "fsdp"), None, None),
        P(("dp", "fsdp"), None, None),
        P(("dp", "fsdp")),
        P(("dp", "fsdp")),
        P(("dp", "fsdp")),
        P(("dp", "fsdp"), None),
        P(("dp", "fsdp")),
        P(),
        P(None, ("dp", "fsdp"), None),
        P(None, ("dp", "fsdp"), None),
        P(("dp", "fsdp")),
        P(("dp", "fsdp")),
        P(None, ("dp", "fsdp"), None),
        P(None, ("dp", "fsdp"), None),
        P(None, ("dp", "fsdp"), None),
        P(None, ("dp", "fsdp"), None),
        P(("dp", "fsdp")),
        P(("dp", "fsdp")),
        P(("dp", "fsdp")),
        P(("dp", "fsdp")),
    )
    out_specs = (
        P(),
        P(),
        P(None, ("dp", "fsdp"), None),
        P(None, ("dp", "fsdp"), None),
        P(None, ("dp", "fsdp"), None),
        P(None, ("dp", "fsdp"), None),
        P(None, ("dp", "fsdp"), None),
        P(None, ("dp", "fsdp"), None),
        P(None, ("dp", "fsdp"), None),
        P(None, ("dp", "fsdp"), None),
        P(("dp", "fsdp")),
        P(("dp", "fsdp")),
        P(("dp", "fsdp")),
        P(("dp", "fsdp")),
        P(("dp", "fsdp")),
        P(("dp", "fsdp")),
        P(("dp", "fsdp")),
        P(("dp", "fsdp")),
        P(),
    )
    return jax.shard_map(body, mesh=mesh, in_specs=in_specs, out_specs=out_specs, check_vma=False)
```
